32 devices in a mesh: grp: 2 (over x), inner: 16 (over z, y, core).
Axes of the slice: x: 2, y: 2, z: 4, core: 2. Of those that a mesh axis runs over, the one named last changes fastest.
Arguments:
- tokens: bfloat16 [128, 8192], P(('grp', 'inner')), parts along dimension 0, may hold values from -6 to 6
- token_scale: bfloat16 [128], P(('grp', 'inner')), parts along dimension 0, may hold values from 0.5 to 2
- gate_weight: bfloat16 [8192, 26624], P(None, 'inner'), may hold values from -0.0625 to 0.0625
- up_weight: bfloat16 [8192, 26624], P(None, 'inner'), may hold values from -0.0625 to 0.0625
- gate_scale: float32 [26624], P('inner'), may hold values from 0.5 to 2
- up_scale: float32 [26624], P('inner'), may hold values from 0.5 to 2
- down_weight: bfloat16 [26624, 8192], P('inner'), may hold values from -0.0390625 to 0.0390625
- down_scale: float32 [8192], replicated, may hold values from 0.5 to 2
Outputs:
- mixed: bfloat16 [128, 8192], P(('grp', 'inner')), parts along dimension 0
The draws below stay inside these ranges and needn't reach their ends.
There are 2 independent parts, one for each index of `grp`. The reference program is written for one: setup_inputs(seed, part) draws one part's arguments, and reference() takes and returns one part's arrays. A program takes and returns all parts, laid end to end along the dimension named above; an argument that names none is the same for every part. Nothing has to cross between parts.
All inputs are finite; a program needn't handle non-finite values.
Results may differ from the reference program's by a relative error of at most 0.0049.
Values may be sent and summed in bfloat16 or wider, within the bound.
A program may use at most 192 MiB of HBM per device.

```python
import math
import jax
import jax.numpy as jnp

D = 8192
FF = 26624
TOKENS = 64


def block_levels(key, shape, shards, least, high):
    level, own = 1.0, jax.random.fold_in(key, 6)
    for dim, shards_of in shards:
        draws = jnp.exp(jax.random.uniform(jax.random.fold_in(own, dim), (shards_of,), jnp.float32, least / len(shards), high / len(shards)))
        level = level * jnp.repeat(draws, shape[dim] // shards_of).reshape([-1 if axis == dim else 1 for axis in range(len(shape))])
    return level


def noise(key, dims, scale, bound, shards=(), dtype=jnp.bfloat16):
    loudness = block_levels(key, dims, shards, -0.22, 0.18) if shards else 1.0
    entries = jax.random.normal(key, dims, jnp.float32) * scale * loudness
    return jnp.minimum(jnp.maximum(entries, -bound), bound).astype(dtype)


def setup_inputs(seed: int = 0, part: int = 0) -> dict:
    arg_keys = jax.random.split(jax.random.key(seed), 9)
    own_keys = jax.random.split(jax.random.fold_in(arg_keys[8], part), 9)
    tokens = noise(own_keys[0], (TOKENS, D), 1.0, 6.0, ((0, 16),))
    token_scale = jnp.clip(jnp.exp(math.log(2.0) - 1.3862944 * jax.random.uniform(own_keys[1], (TOKENS,), jnp.float32) ** block_levels(own_keys[1], (TOKENS,), ((0, 16),), -0.2, 0.2)), 0.5, 2.0).astype(jnp.bfloat16)
    gate_weight = noise(arg_keys[2], (D, FF), D ** -0.5, 0.0625, ((1, 16),))
    up_weight = noise(arg_keys[3], (D, FF), D ** -0.5, 0.0625, ((1, 16),))
    gate_scale = jnp.clip(jnp.exp(math.log(2.0) - 1.3862944 * jax.random.uniform(arg_keys[4], (FF,), jnp.float32) ** block_levels(arg_keys[4], (FF,), ((0, 16),), -0.2, 0.2)), 0.5, 2.0)
    up_scale = jnp.clip(jnp.exp(math.log(2.0) - 1.3862944 * jax.random.uniform(arg_keys[5], (FF,), jnp.float32) ** block_levels(arg_keys[5], (FF,), ((0, 16),), -0.2, 0.2)), 0.5, 2.0)
    down_weight = noise(arg_keys[6], (FF, D), FF ** -0.5, 0.0390625, ((0, 16),))
    down_scale = jnp.clip(jnp.exp(jax.random.uniform(arg_keys[7], (D,), jnp.float32, math.log(0.5), math.log(2.0))), 0.5, 2.0)
    return {"tokens": tokens, "token_scale": token_scale, "gate_weight": gate_weight, "up_weight": up_weight, "gate_scale": gate_scale, "up_scale": up_scale, "down_weight": down_weight, "down_scale": down_scale}


def reference(tokens, token_scale, gate_weight, up_weight, gate_scale, up_scale, down_weight, down_scale):
    factor = token_scale.astype(jnp.float32)[:, None]
    gate = jnp.dot(tokens, gate_weight, preferred_element_type=jnp.float32) * factor * gate_scale[None, :]
    up = jnp.dot(tokens, up_weight, preferred_element_type=jnp.float32) * factor * up_scale[None, :]
    hidden = (jax.nn.silu(gate) * up).astype(jnp.bfloat16)
    total = jnp.dot(hidden, down_weight, preferred_element_type=jnp.float32)
    return (total * down_scale[None, :]).astype(jnp.bfloat16)
```

```python
import jax
import jax.numpy as jnp
from jax import lax
from jax.experimental import pallas as pl
from jax.experimental.pallas import tpu as pltpu
from jax.sharding import PartitionSpec as P

MESH = pl.DeviceIdType.MESH
F32, BF16 = jnp.float32, jnp.bfloat16

FOLD = 4
TC = 4
NC = 8
NB = 5
Z, Y = 4, 2


def plain(
    tokens, token_scale, gate_weight, up_weight, gate_scale, up_scale, down_weight, down_scale
):
    pieces = lax.all_gather((tokens, token_scale), "inner", axis=0, tiled=True)
    token_codes = pieces[0]
    factor = pieces[1].astype(F32)[:, None]
    gate = (
        jnp.dot(token_codes, gate_weight, preferred_element_type=F32)
        * factor
        * gate_scale[None, :]
    )
    up = (
        jnp.dot(token_codes, up_weight, preferred_element_type=F32)
        * factor
        * up_scale[None, :]
    )
    hidden = (jax.nn.silu(gate) * up).astype(BF16)
    summed = lax.psum_scatter(
        jnp.dot(hidden, down_weight, preferred_element_type=F32),
        "inner",
        scatter_dimension=0,
        tiled=True,
    )
    return (summed * down_scale[None, :]).astype(BF16)


def kernel(
    tok, gw, uw, gs, us, dw, out,
    g0, g1, g2, g3, left, fac, gbuf, ubuf, dbuf, acc_g, acc_u, hid, full,
    part, s1s, s1r, part2, s2s, s2r, part3, s3s, s3r,
    wsem, dsem, zs, zr, h1s, h1r, h2s, h2r, cs, cr, hs, hr, r1s, r1r, r2s, r2r, r3s, r3r,
):
    x = lax.axis_index("grp")
    inner = lax.axis_index("inner")
    core, y, z = inner % 2, (inner // 2) % 2, inner // 4
    xf, yf = 1 - x, 1 - y

    def dev(xx, zz, yy, cc):
        return (xx, (zz * Y + yy) * 2 + cc)

    gathered = (g0, g1, g2, g3)
    width = fac.shape[1]
    kw = (tok.shape[1] - width) // TC
    half = hid.shape[3]
    ff = full.shape[2]
    rest = ff - half
    ncol = dbuf.shape[2]
    off = pl.multiple_of(x * rest, 128)

    def wcopy(c, which):
        src, dst = ((gw, gbuf), (uw, ubuf))[which]
        return pltpu.make_async_copy(
            src.at[:, pl.ds(c * kw, kw), pl.ds(off, half)], dst.at[c], wsem.at[which, c]
        )

    def dcopy(n):
        return pltpu.make_async_copy(
            dw.at[:, pl.ds(n * ncol, ncol)], dbuf.at[n % NB], dsem.at[n]
        )

    for c in range(TC):
        wcopy(c, 0).start()
        wcopy(c, 1).start()
    for n in range(NB):
        dcopy(n).start()

    col = x * 2 + y
    rows = pl.ds(pl.multiple_of(z * 16, 16), 16)
    g0[core, col, rows, pl.ds(0, kw)] = tok[:, pl.ds(0, kw)]
    g0[core, col, rows, pl.ds(kw, width)] = tok[:, pl.ds(TC * kw, width)]
    for c in range(1, TC):
        gathered[c][core, col, rows, :] = tok[:, pl.ds(c * kw, kw)]

    peers = [dev(x, (z + d) % Z, y, core) for d in range(1, Z)]
    xdev, ydev, cdev = dev(xf, z, y, core), dev(x, z, yf, core), dev(x, z, y, 1 - core)
    barrier = pltpu.get_barrier_semaphore()
    for peer in peers + [xdev, ydev, cdev]:
        pl.semaphore_signal(barrier, inc=1, device_id=peer, device_id_type=MESH)
    pl.semaphore_wait(barrier, Z + 2)

    def remote(src, dst, ssem, rsem, peer):
        return pltpu.make_async_remote_copy(
            src_ref=src, dst_ref=dst, send_sem=ssem, recv_sem=rsem,
            device_id=peer, device_id_type=MESH,
        )

    n1x, n1y = (1 - core) * xf + core * x, (1 - core) * y + core * yf
    n2x, n2y = (1 - core) * x + core * xf, (1 - core) * yf + core * y
    n1, n2 = dev(n1x, z, n1y, core), dev(n2x, z, n2y, core)
    n1col, n2col, diag = n1x * 2 + n1y, n2x * 2 + n2y, xf * 2 + yf

    def zsend(c, d):
        block = gathered[c].at[core, col, rows]
        return remote(block, block, zs.at[c, d - 1], zr.at[c, d - 1], peers[d - 1])

    def zrecv(c, d):
        src = pl.ds(pl.multiple_of(((z + Z - d) % Z) * 16, 16), 16)
        block = gathered[c].at[core, col, src]
        return remote(block, block, zs.at[c, d - 1], zr.at[c, d - 1], peers[d - 1])

    def hop1(c, which):
        block = gathered[c].at[core, which]
        return remote(block, block, h1s.at[c], h1r.at[c], n1)

    def hop2(c, i, which):
        block = gathered[c].at[core, which]
        return remote(block, block, h2s.at[c, i], h2r.at[c, i], n2)

    def cross(c, which):
        block = gathered[c].at[which]
        return remote(block, block, cs.at[c], cr.at[c], cdev)

    for c in range(TC):
        for d in range(1, Z):
            zsend(c, d).start()

    o = lax.broadcasted_iota(jnp.int32, (256, 256), 0)
    i = lax.broadcasted_iota(jnp.int32, (256, 256), 1)
    target = ((o & 63) >> 2) * 16 + (o & 3) * FOLD + (o >> 6)
    perm = jnp.where(i == target, 1.0, 0.0).astype(BF16)

    def compute(c):
        for cc in range(2):
            codes = gathered[c][cc].reshape(256, gathered[c].shape[3])
            moved = jnp.dot(perm, codes, preferred_element_type=F32)
            if c == 0:
                fac[pl.ds(cc * 64, 64), :] = moved[:64, kw:]
            for q in range(FOLD):
                left[q, pl.ds(cc * 64, 64), :] = moved[q * 64:(q + 1) * 64, :kw].astype(BF16)
        wcopy(c, 0).wait()
        wcopy(c, 1).wait()
        if c == 0:
            acc_g[...] = jnp.zeros_like(acc_g)
            acc_u[...] = jnp.zeros_like(acc_u)

        def step(q, carry):
            acc_g[...] += jnp.dot(left[q], gbuf[c, q], preferred_element_type=F32)
            acc_u[...] += jnp.dot(left[q], ubuf[c, q], preferred_element_type=F32)
            return carry

        lax.fori_loop(0, FOLD, step, 0)

    for s in range(TC + 3):
        if s < TC:
            for d in range(1, Z):
                zrecv(s, d).wait_recv()
            hop1(s, col).start()
        if 0 <= s - 1 < TC:
            hop1(s - 1, n1col).wait_recv()
            hop2(s - 1, 0, col).start()
            hop2(s - 1, 1, n1col).start()
        if 0 <= s - 2 < TC:
            hop2(s - 2, 0, n2col).wait_recv()
            hop2(s - 2, 1, diag).wait_recv()
            cross(s - 2, core).start()
        if 0 <= s - 3 < TC:
            cross(s - 3, 1 - core).wait_recv()
            compute(s - 3)

    factor = fac[:, 0:1]
    gate = acc_g[...] * factor * gs[:, pl.ds(off, half)]
    up = acc_u[...] * factor * us[:, pl.ds(off, half)]
    hidden = (gate / (1.0 + jnp.exp(-gate)) * up).astype(BF16)
    hid[...] = hidden.reshape(2, 2, 32, half)

    def exchange(which):
        return remote(
            hid.at[:, 1 - which, :, pl.ds(pl.multiple_of(which * (half - rest), 128), rest)],
            full.at[:, :, pl.ds(pl.multiple_of(which * half, 128), rest)],
            hs, hr, xdev,
        )

    exchange(x).start()
    full[:, :, pl.ds(off, half)] = hid[:, x]
    exchange(xf).wait_recv()

    def r1(n):
        return remote(s1s.at[n], s1r.at[n], r1s.at[n], r1r.at[n], cdev)

    def r2(n):
        return remote(s2s.at[n], s2r.at[n], r2s.at[n], r2r.at[n], ydev)

    def r3(n, d):
        return remote(
            s3s.at[n, (z + d) % Z], s3r.at[n, d - 1], r3s.at[n, d - 1], r3r.at[n, d - 1],
            peers[d - 1],
        )

    cw = ncol // FOLD
    for s in range(NC + 3):
        if s < NC:
            n = s
            dcopy(n).wait()
            product = jnp.dot(
                full[...].reshape(64, ff), dbuf[n % NB], preferred_element_type=F32
            )
            part[n] = product.reshape(2, 32, ncol)
            s1s[n] = part[n, 1 - core].astype(BF16)
            r1(n).start()
            if n + NB < NC:
                dcopy(n + NB).start()
        if 0 <= s - 1 < NC:
            n = s - 1
            r1(n).wait_recv()
            part2[n] = (part[n, core] + s1r[n].astype(F32)).reshape(2, 16, ncol)
            s2s[n] = part2[n, 1 - y].astype(BF16)
            r2(n).start()
        if 0 <= s - 2 < NC:
            n = s - 2
            r2(n).wait_recv()
            v = part2[n, y] + s2r[n].astype(F32)
            for zz in range(Z):
                block = jnp.concatenate(
                    [v[zz * 4:(zz + 1) * 4, j * cw:(j + 1) * cw] for j in range(FOLD)], axis=0
                )
                part3[n, zz] = block
                s3s[n, zz] = block.astype(BF16)
            for d in range(1, Z):
                r3(n, d).start()
        if 0 <= s - 3 < NC:
            n = s - 3
            for d in range(1, Z):
                r3(n, d).wait_recv()
            total = part3[n, z]
            for d in range(1, Z):
                total += s3r[n, d - 1].astype(F32)
            out[n] = total

    for c in range(TC):
        for d in range(1, Z):
            zsend(c, d).wait_send()
        hop1(c, col).wait_send()
        hop2(c, 0, col).wait_send()
        hop2(c, 1, n1col).wait_send()
        cross(c, core).wait_send()
    exchange(x).wait_send()
    for n in range(NC):
        r1(n).wait_send()
        r2(n).wait_send()
        for d in range(1, Z):
            r3(n, d).wait_send()


def local(
    tokens, token_scale, gate_weight, up_weight, gate_scale, up_scale, down_weight, down_scale
):
    rows, depth = tokens.shape
    ff = gate_weight.shape[1]
    half = (ff // 128 + 1) // 2 * 128
    kw = depth // FOLD // TC
    ncol = depth // NC
    lanes = 128
    codes = jnp.concatenate(
        [
            tokens.reshape(rows * FOLD, depth // FOLD),
            jnp.broadcast_to(token_scale[:, None, None], (rows, FOLD, lanes)).reshape(-1, lanes),
        ],
        axis=1,
    )
    vmem = pl.BlockSpec(memory_space=pltpu.VMEM)
    hbm = pl.BlockSpec(memory_space=pl.ANY)
    dma = pltpu.SemaphoreType.DMA
    cw = ncol // FOLD
    sums = pl.pallas_call(
        kernel,
        out_shape=jax.ShapeDtypeStruct((NC, 16, cw), F32),
        in_specs=[vmem, hbm, hbm, vmem, vmem, hbm],
        out_specs=vmem,
        scratch_shapes=[
            pltpu.VMEM((2, 4, 64, kw + lanes), BF16),
            pltpu.VMEM((2, 4, 64, kw), BF16),
            pltpu.VMEM((2, 4, 64, kw), BF16),
            pltpu.VMEM((2, 4, 64, kw), BF16),
            pltpu.VMEM((FOLD, 128, kw), BF16),
            pltpu.VMEM((128, lanes), F32),
            pltpu.VMEM((TC, FOLD, kw, half), BF16),
            pltpu.VMEM((TC, FOLD, kw, half), BF16),
            pltpu.VMEM((NB, ff, ncol), BF16),
            pltpu.VMEM((128, half), F32),
            pltpu.VMEM((128, half), F32),
            pltpu.VMEM((2, 2, 32, half), BF16),
            pltpu.VMEM((2, 32, ff), BF16),
            pltpu.VMEM((NC, 2, 32, ncol), F32),
            pltpu.VMEM((NC, 32, ncol), BF16),
            pltpu.VMEM((NC, 32, ncol), BF16),
            pltpu.VMEM((NC, 2, 16, ncol), F32),
            pltpu.VMEM((NC, 16, ncol), BF16),
            pltpu.VMEM((NC, 16, ncol), BF16),
            pltpu.VMEM((NC, Z, 16, cw), F32),
            pltpu.VMEM((NC, Z, 16, cw), BF16),
            pltpu.VMEM((NC, Z - 1, 16, cw), BF16),
            dma((2, TC)),
            dma((NC,)),
            dma((TC, Z - 1)),
            dma((TC, Z - 1)),
            dma((TC,)),
            dma((TC,)),
            dma((TC, 2)),
            dma((TC, 2)),
            dma((TC,)),
            dma((TC,)),
            dma,
            dma,
            dma((NC,)),
            dma((NC,)),
            dma((NC,)),
            dma((NC,)),
            dma((NC, Z - 1)),
            dma((NC, Z - 1)),
        ],
        compiler_params=pltpu.CompilerParams(
            collective_id=0, has_side_effects=True, vmem_limit_bytes=62 << 20
        ),
        name="ffn",
    )(
        codes,
        gate_weight.reshape(FOLD, depth // FOLD, ff),
        up_weight.reshape(FOLD, depth // FOLD, ff),
        gate_scale[None, :],
        up_scale[None, :],
        down_weight,
    )
    scale = down_scale.reshape(NC, FOLD, 1, cw)
    mixed = (sums.reshape(NC, FOLD, rows, cw) * scale).astype(BF16)
    return mixed.transpose(2, 0, 1, 3).reshape(rows, depth)


def dispatch(tokens, token_scale, gate_weight, *others):
    rows, depth = tokens.shape
    ff = gate_weight.shape[1]
    fits = (
        lax.axis_size("grp") == 2
        and lax.axis_size("inner") == 2 * Y * Z
        and rows == 4
        and depth % (FOLD * TC * 128) == 0
        and depth % (NC * FOLD * 128) == 0
        and ff % 128 == 0
        and ff > 128
    )
    form = local if fits else plain
    return form(tokens, token_scale, gate_weight, *others)


def solution(mesh):
    return jax.shard_map(
        dispatch,
        mesh=mesh,
        in_specs=(
            P(("grp", "inner"), None),
            P(("grp", "inner")),
            P(None, "inner"),
            P(None, "inner"),
            P("inner"),
            P("inner"),
            P("inner", None),
            P(),
        ),
        out_specs=P(("grp", "inner"), None),
        check_vma=False,
    )
```

```python
import jax
import jax.numpy as jnp
from jax import lax
from jax.experimental import pallas as pl
from jax.experimental.pallas import tpu as pltpu
from jax.sharding import PartitionSpec as P

MESH = pl.DeviceIdType.MESH
F32, BF16 = jnp.float32, jnp.bfloat16

FOLD = 4
TC = 4
NC = 8
NB = 6
Z, Y = 4, 2
LAG = (2, 5, 8)


def plain(
    tokens, token_scale, gate_weight, up_weight, gate_scale, up_scale, down_weight, down_scale
):
    pieces = lax.all_gather((tokens, token_scale), "inner", axis=0, tiled=True)
    token_codes = pieces[0]
    factor = pieces[1].astype(F32)[:, None]
    gate = (
        jnp.dot(token_codes, gate_weight, preferred_element_type=F32)
        * factor
        * gate_scale[None, :]
    )
    up = (
        jnp.dot(token_codes, up_weight, preferred_element_type=F32)
        * factor
        * up_scale[None, :]
    )
    hidden = (jax.nn.silu(gate) * up).astype(BF16)
    summed = lax.psum_scatter(
        jnp.dot(hidden, down_weight, preferred_element_type=F32),
        "inner",
        scatter_dimension=0,
        tiled=True,
    )
    return (summed * down_scale[None, :]).astype(BF16)


def kernel(
    tok, gw, uw, gs, us, dw, out,
    g0, g1, g2, g3, left, fac, gbuf, ubuf, dbuf, acc_g, acc_u, hid, full,
    part, s1s, s1r, part2, s2s, s2r, part3, s3s, s3r,
    wsem, dsem, zs, zr, h1s, h1r, cs, cr, hs, hr, r1s, r1r, r2s, r2r, r3s, r3r,
):
    x = lax.axis_index("grp")
    inner = lax.axis_index("inner")
    core, y, z = inner % 2, (inner // 2) % 2, inner // 4
    xf, yf = 1 - x, 1 - y

    def dev(xx, zz, yy, cc):
        return (xx, (zz * Y + yy) * 2 + cc)

    gathered = (g0, g1, g2, g3)
    width = fac.shape[1]
    kw = (tok.shape[1] - width) // TC
    half = hid.shape[3]
    ff = full.shape[2]
    rest = ff - half
    ncol = dbuf.shape[2]
    off = pl.multiple_of(x * rest, 128)

    def wcopy(c, which):
        src, dst = ((gw, gbuf), (uw, ubuf))[which]
        return pltpu.make_async_copy(
            src.at[:, pl.ds(c * kw, kw), pl.ds(off, half)], dst.at[c], wsem.at[which, c]
        )

    def dcopy(n):
        return pltpu.make_async_copy(
            dw.at[:, pl.ds(n * ncol, ncol)], dbuf.at[n % NB], dsem.at[n]
        )

    for c in range(TC):
        wcopy(c, 0).start()
        wcopy(c, 1).start()
    for n in range(NB):
        dcopy(n).start()

    col = x * 2 + y
    rows = pl.ds(pl.multiple_of(z * 16, 16), 16)
    g0[core, col, rows, pl.ds(0, kw)] = tok[:, pl.ds(0, kw)]
    g0[core, col, rows, pl.ds(kw, width)] = tok[:, pl.ds(TC * kw, width)]
    for c in range(1, TC):
        gathered[c][core, col, rows, :] = tok[:, pl.ds(c * kw, kw)]

    peers = [dev(x, (z + d) % Z, y, core) for d in range(1, Z)]
    xdev, ydev, cdev = dev(xf, z, y, core), dev(x, z, yf, core), dev(x, z, y, 1 - core)
    ddev = dev(xf, z, yf, core)
    barrier = pltpu.get_barrier_semaphore()
    for peer in peers + [xdev, ydev, ddev, cdev]:
        pl.semaphore_signal(barrier, inc=1, device_id=peer, device_id_type=MESH)
    pl.semaphore_wait(barrier, Z + 3)

    def remote(src, dst, ssem, rsem, peer):
        return pltpu.make_async_remote_copy(
            src_ref=src, dst_ref=dst, send_sem=ssem, recv_sem=rsem,
            device_id=peer, device_id_type=MESH,
        )

    plane = [(xdev, xf * 2 + y), (ydev, x * 2 + yf), (ddev, xf * 2 + yf)]

    def zsend(c, d):
        block = gathered[c].at[core, col, rows]
        return remote(block, block, zs.at[c, d - 1], zr.at[c, d - 1], peers[d - 1])

    def zrecv(c, d):
        src = pl.ds(pl.multiple_of(((z + Z - d) % Z) * 16, 16), 16)
        block = gathered[c].at[core, col, src]
        return remote(block, block, zs.at[c, d - 1], zr.at[c, d - 1], peers[d - 1])

    def spread(c, k, which):
        block = gathered[c].at[core, which]
        return remote(block, block, h1s.at[c, k], h1r.at[c, k], plane[k][0])

    def cross(c, which):
        block = gathered[c].at[which]
        return remote(block, block, cs.at[c], cr.at[c], cdev)

    for c in range(TC):
        for d in range(1, Z):
            zsend(c, d).start()

    o = lax.broadcasted_iota(jnp.int32, (256, 256), 0)
    i = lax.broadcasted_iota(jnp.int32, (256, 256), 1)
    target = ((o & 63) >> 2) * 16 + (o & 3) * FOLD + (o >> 6)
    perm = jnp.where(i == target, 1.0, 0.0).astype(BF16)

    def compute(c):
        for cc in range(2):
            codes = gathered[c][cc].reshape(256, gathered[c].shape[3])
            moved = jnp.dot(perm, codes, preferred_element_type=F32)
            if c == 0:
                fac[pl.ds(cc * 64, 64), :] = moved[:64, kw:]
            for q in range(FOLD):
                left[q, pl.ds(cc * 64, 64), :] = moved[q * 64:(q + 1) * 64, :kw].astype(BF16)
        wcopy(c, 0).wait()
        wcopy(c, 1).wait()
        if c == 0:
            acc_g[...] = jnp.zeros_like(acc_g)
            acc_u[...] = jnp.zeros_like(acc_u)

        def step(q, carry):
            acc_g[...] += jnp.dot(left[q], gbuf[c, q], preferred_element_type=F32)
            acc_u[...] += jnp.dot(left[q], ubuf[c, q], preferred_element_type=F32)
            return carry

        lax.fori_loop(0, FOLD, step, 0)

    for c in range(TC):
        for d in range(1, Z):
            zrecv(c, d).wait_recv()
        for k in range(3):
            spread(c, k, col).start()
    for s in range(TC + 1):
        if s < TC:
            for k in range(3):
                spread(s, k, plane[k][1]).wait_recv()
            cross(s, core).start()
        if s >= 1:
            cross(s - 1, 1 - core).wait_recv()
            compute(s - 1)

    factor = fac[:, 0:1]
    gate = acc_g[...] * factor * jnp.where(x == 0, gs[0:half], gs[rest:ff])[None, :]
    up = acc_u[...] * factor * jnp.where(x == 0, us[0:half], us[rest:ff])[None, :]
    hidden = (gate / (1.0 + jnp.exp(-gate)) * up).astype(BF16)
    hid[...] = hidden.reshape(2, 2, 32, half)

    def exchange(which):
        return remote(
            hid.at[:, 1 - which, :, pl.ds(pl.multiple_of(which * (half - rest), 128), rest)],
            full.at[:, :, pl.ds(pl.multiple_of(which * half, 128), rest)],
            hs, hr, xdev,
        )

    exchange(x).start()
    full[:, :, pl.ds(off, half)] = hid[:, x]
    own = hid[:, x].reshape(64, half)
    for n in range(NB):
        dcopy(n).wait()
        product = jnp.dot(own, dbuf[n, pl.ds(off, half), :], preferred_element_type=F32)
        part[n] = product.reshape(2, 32, ncol)
    exchange(xf).wait_recv()
    far = pl.ds(pl.multiple_of((1 - x) * half, 128), rest)

    def r1(n):
        return remote(s1s.at[n], s1r.at[n], r1s.at[n], r1r.at[n], cdev)

    def r2(n):
        return remote(s2s.at[n], s2r.at[n], r2s.at[n], r2r.at[n], ydev)

    def r3(n, d):
        return remote(
            s3s.at[n, (z + d) % Z], s3r.at[n, d - 1], r3s.at[n, d - 1], r3r.at[n, d - 1],
            peers[d - 1],
        )

    cw = ncol // FOLD
    for s in range(NC + LAG[2]):
        if s < NC:
            n = s
            if n < NB:
                product = jnp.dot(
                    full[:, :, far].reshape(64, rest), dbuf[n, far, :],
                    preferred_element_type=F32,
                )
                part[n] += product.reshape(2, 32, ncol)
            else:
                dcopy(n).wait()
                product = jnp.dot(
                    full[...].reshape(64, ff), dbuf[n % NB], preferred_element_type=F32
                )
                part[n] = product.reshape(2, 32, ncol)
            s1s[n] = part[n, 1 - core].astype(BF16)
            r1(n).start()
            if n + NB < NC:
                dcopy(n + NB).start()
        if 0 <= s - LAG[0] < NC:
            n = s - LAG[0]
            r1(n).wait_recv()
            part2[n] = (part[n, core] + s1r[n].astype(F32)).reshape(2, 16, ncol)
            s2s[n] = part2[n, 1 - y].astype(BF16)
            r2(n).start()
        if 0 <= s - LAG[1] < NC:
            n = s - LAG[1]
            r2(n).wait_recv()
            v = part2[n, y] + s2r[n].astype(F32)
            for zz in range(Z):
                block = jnp.concatenate(
                    [v[zz * 4:(zz + 1) * 4, j * cw:(j + 1) * cw] for j in range(FOLD)], axis=0
                )
                part3[n, zz] = block
                s3s[n, zz] = block.astype(BF16)
            for d in range(1, Z):
                r3(n, d).start()
        if 0 <= s - LAG[2] < NC:
            n = s - LAG[2]
            for d in range(1, Z):
                r3(n, d).wait_recv()
            total = part3[n, z]
            for d in range(1, Z):
                total += s3r[n, d - 1].astype(F32)
            out[n] = total

    for c in range(TC):
        for d in range(1, Z):
            zsend(c, d).wait_send()
        for k in range(3):
            spread(c, k, col).wait_send()
        cross(c, core).wait_send()
    exchange(x).wait_send()
    for n in range(NC):
        r1(n).wait_send()
        r2(n).wait_send()
        for d in range(1, Z):
            r3(n, d).wait_send()


def local(
    tokens, token_scale, gate_weight, up_weight, gate_scale, up_scale, down_weight, down_scale
):
    rows, depth = tokens.shape
    ff = gate_weight.shape[1]
    half = (ff // 128 + 1) // 2 * 128
    kw = depth // FOLD // TC
    ncol = depth // NC
    lanes = 128
    codes = jnp.concatenate(
        [
            tokens.reshape(rows * FOLD, depth // FOLD),
            jnp.broadcast_to(token_scale[:, None, None], (rows, FOLD, lanes)).reshape(-1, lanes),
        ],
        axis=1,
    )
    vmem = pl.BlockSpec(memory_space=pltpu.VMEM)
    hbm = pl.BlockSpec(memory_space=pl.ANY)
    dma = pltpu.SemaphoreType.DMA
    cw = ncol // FOLD
    sums = pl.pallas_call(
        kernel,
        out_shape=jax.ShapeDtypeStruct((NC, 16, cw), F32),
        in_specs=[vmem, hbm, hbm, vmem, vmem, hbm],
        out_specs=vmem,
        scratch_shapes=[
            pltpu.VMEM((2, 4, 64, kw + lanes), BF16),
            pltpu.VMEM((2, 4, 64, kw), BF16),
            pltpu.VMEM((2, 4, 64, kw), BF16),
            pltpu.VMEM((2, 4, 64, kw), BF16),
            pltpu.VMEM((FOLD, 128, kw), BF16),
            pltpu.VMEM((128, lanes), F32),
            pltpu.VMEM((TC, FOLD, kw, half), BF16),
            pltpu.VMEM((TC, FOLD, kw, half), BF16),
            pltpu.VMEM((NB, ff, ncol), BF16),
            pltpu.VMEM((128, half), F32),
            pltpu.VMEM((128, half), F32),
            pltpu.VMEM((2, 2, 32, half), BF16),
            pltpu.VMEM((2, 32, ff), BF16),
            pltpu.VMEM((NC, 2, 32, ncol), F32),
            pltpu.VMEM((NC, 32, ncol), BF16),
            pltpu.VMEM((NC, 32, ncol), BF16),
            pltpu.VMEM((NC, 2, 16, ncol), F32),
            pltpu.VMEM((NC, 16, ncol), BF16),
            pltpu.VMEM((NC, 16, ncol), BF16),
            pltpu.VMEM((NC, Z, 16, cw), F32),
            pltpu.VMEM((NC, Z, 16, cw), BF16),
            pltpu.VMEM((NC, Z - 1, 16, cw), BF16),
            dma((2, TC)),
            dma((NC,)),
            dma((TC, Z - 1)),
            dma((TC, Z - 1)),
            dma((TC, 3)),
            dma((TC, 3)),
            dma((TC,)),
            dma((TC,)),
            dma,
            dma,
            dma((NC,)),
            dma((NC,)),
            dma((NC,)),
            dma((NC,)),
            dma((NC, Z - 1)),
            dma((NC, Z - 1)),
        ],
        compiler_params=pltpu.CompilerParams(
            collective_id=0, has_side_effects=True, vmem_limit_bytes=62 << 20
        ),
        name="ffn",
    )(
        codes,
        gate_weight.reshape(FOLD, depth // FOLD, ff),
        up_weight.reshape(FOLD, depth // FOLD, ff),
        gate_scale,
        up_scale,
        down_weight,
    )
    scale = down_scale.reshape(NC, FOLD, 1, cw)
    mixed = (sums.reshape(NC, FOLD, rows, cw) * scale).astype(BF16)
    return mixed.transpose(2, 0, 1, 3).reshape(rows, depth)


def dispatch(tokens, token_scale, gate_weight, *others):
    rows, depth = tokens.shape
    ff = gate_weight.shape[1]
    fits = (
        lax.axis_size("grp") == 2
        and lax.axis_size("inner") == 2 * Y * Z
        and rows == 4
        and depth % (FOLD * TC * 128) == 0
        and depth % (NC * FOLD * 128) == 0
        and ff % 128 == 0
        and ff > 128
    )
    form = local if fits else plain
    return form(tokens, token_scale, gate_weight, *others)


def solution(mesh):
    return jax.shard_map(
        dispatch,
        mesh=mesh,
        in_specs=(
            P(("grp", "inner"), None),
            P(("grp", "inner")),
            P(None, "inner"),
            P(None, "inner"),
            P("inner"),
            P("inner"),
            P("inner", None),
            P(),
        ),
        out_specs=P(("grp", "inner"), None),
        check_vma=False,
    )
```
